512 devices in a mesh: sp: 32 (over x_lo, z), fsdp: 8 (over y, core), dp: 2 (over x_hi).
Axes of the slice: x: 4 (x_hi: 2, x_lo: 2; x = x_hi * 2 + x_lo), y: 4, z: 16, core: 2. Of those that a mesh axis runs over, the one named last changes fastest.
Arguments:
- tokens: bfloat16 [16, 4096, 1152], P(('fsdp', 'dp'), 'sp'), may hold values from -6 to 6
- key_proj: bfloat16 [16, 4096, 4096], P(('fsdp', 'dp'), 'sp'), may hold values from -6 to 6
- key_cot: bfloat16 [16, 4096, 4096], P(('fsdp', 'dp'), None, 'sp'), may hold values from -6 to 6
- gate_cot: bfloat16 [16, 4096, 4096], P(('fsdp', 'dp'), None, 'sp'), may hold values from -6 to 6
- key_weight: bfloat16 [1152, 4096], P('fsdp'), may hold values from -0.1875 to 0.1875
- gate_down: bfloat16 [1152, 128], P('fsdp'), may hold values from -0.1875 to 0.1875
- gate_up: bfloat16 [128, 4096], P('fsdp'), may hold values from -0.5 to 0.5
- gate_bias: float32 [4096], replicated, may hold values from -4 to 4
- conv_weight: bfloat16 [4, 4096], replicated, may hold values from -3 to 3
Outputs:
- input_grad: bfloat16 [16, 4096, 1152], P(('fsdp', 'dp'), 'sp')
- down_grad: float32 [1152, 128], P('fsdp')
- up_grad: float32 [128, 4096], P('fsdp', 'sp')
- conv_grad: float32 [4, 4096], P(None, 'fsdp')
- bias_grad: float32 [4096], P('fsdp')
The draws below stay inside these ranges and needn't reach their ends.
All inputs are finite; a program needn't handle non-finite values.
Results may differ from the reference program's by a relative error of at most 0.007.
Values may be sent and summed in bfloat16 or wider, within the bound.
No kernel may reach another device: no remote copies, remote signals or barrier semaphores. Data moves between devices by JAX's collectives and lax.ppermute only.
A program may use at most 64 MiB of HBM per device.

```python
import jax
import jax.numpy as jnp
from jax import lax

DW = 1152
RANK = 128
CONV = 4
HD = 4096
LEN = 4096
SEQS = 16


def block_levels(key, extent, pieces, least, top_value):
    loudness = 1.0
    for dim, shards_of in pieces:
        steps = jax.random.uniform(jax.random.fold_in(jax.random.fold_in(key, 6), dim), (shards_of,), jnp.float32, least / len(pieces), top_value / len(pieces))
        loudness = loudness * jnp.repeat(jnp.exp(steps), extent[dim] // shards_of).reshape((-1,) + (1,) * (len(extent) - 1 - dim))
    return loudness


def scatter_about(rng, shape, spread, bound, pieces=(), held_as=jnp.bfloat16):
    level = block_levels(rng, shape, pieces, -0.22, 0.18) if pieces else 1.0
    drawn = jax.random.normal(rng, shape, jnp.float32) * spread * level
    return jnp.minimum(jnp.maximum(drawn, -bound), bound).astype(held_as)


def setup_inputs(seed: int = 0) -> dict:
    key_list = jax.random.split(jax.random.key(seed), 10)
    return {
        "tokens": scatter_about(key_list[0], (SEQS, LEN, DW), 1.0, 6.0, ((0, 16), (1, 32))),
        "key_proj": scatter_about(key_list[1], (SEQS, LEN, HD), 1.0, 6.0, ((0, 16), (1, 32))),
        "key_cot": scatter_about(key_list[2], (SEQS, LEN, HD), 1.0, 6.0, ((0, 16), (2, 32))),
        "gate_cot": scatter_about(key_list[3], (SEQS, LEN, HD), 1.0, 6.0, ((0, 16), (2, 32))),
        "key_weight": scatter_about(key_list[4], (DW, HD), DW ** -0.5, 0.1875, ((0, 8),)),
        "gate_down": scatter_about(key_list[5], (DW, RANK), DW ** -0.5, 0.1875, ((0, 8),)),
        "gate_up": scatter_about(key_list[6], (RANK, HD), RANK ** -0.5, 0.5, ((0, 8),)),
        "gate_bias": scatter_about(key_list[7], (HD,), 1.0, 4.0, (), jnp.float32),
        "conv_weight": scatter_about(key_list[8], (CONV, HD), 0.5, 3.0),
    }


def silu_slope(values):
    squashed = jax.nn.sigmoid(values)
    return squashed * (1.0 + values * (1.0 - squashed))


def one_window(operands, key_weight, gate_down, gate_up, gate_bias, conv_weight):
    tokens, key_proj, key_cot, gate_cot = operands
    length = tokens.shape[0]
    margin = CONV - 1
    conv_taps = conv_weight.astype(jnp.float32)
    earlier = jnp.concatenate([jnp.zeros((margin, key_proj.shape[1]), jnp.float32), key_proj.astype(jnp.float32)], axis=0)
    conv_out = sum(conv_taps[offset] * earlier[margin - offset: margin - offset + length] for offset in range(CONV))
    slope_grad = (key_cot.astype(jnp.float32) * silu_slope(conv_out)).astype(jnp.bfloat16)
    later_rows = jnp.concatenate([slope_grad.astype(jnp.float32), jnp.zeros((margin, key_proj.shape[1]), jnp.float32)], axis=0)
    proj_grad = sum(conv_taps[offset] * later_rows[offset: offset + length] for offset in range(CONV)).astype(jnp.bfloat16)
    conv_sum = jnp.stack([jnp.sum(later_rows[:length] * earlier[margin - offset: margin - offset + length], axis=0) for offset in range(CONV)])
    latent = jnp.dot(tokens, gate_down, preferred_element_type=jnp.float32).astype(jnp.bfloat16)
    logits = jnp.dot(latent, gate_up, preferred_element_type=jnp.float32) + gate_bias
    gate_grad = (-gate_cot.astype(jnp.float32) * jax.nn.sigmoid(logits)).astype(jnp.bfloat16)
    bias_sum = jnp.sum(gate_grad.astype(jnp.float32), axis=0)
    up_sum = jnp.dot(latent.T, gate_grad, preferred_element_type=jnp.float32)
    latent_grad = jnp.dot(gate_grad, gate_up.T, preferred_element_type=jnp.float32).astype(jnp.bfloat16)
    down_sum = jnp.dot(tokens.T, latent_grad, preferred_element_type=jnp.float32)
    input_grad = (jnp.dot(proj_grad, key_weight.T, preferred_element_type=jnp.float32)
                  + jnp.dot(latent_grad, gate_down.T, preferred_element_type=jnp.float32)).astype(jnp.bfloat16)
    return input_grad, down_sum, up_sum, conv_sum, bias_sum


def reference(tokens, key_proj, key_cot, gate_cot, key_weight, gate_down, gate_up, gate_bias, conv_weight):
    def window_fn(operands):
        return one_window(operands, key_weight, gate_down, gate_up, gate_bias, conv_weight)

    input_grad, down_sum, up_sum, conv_sum, bias_sum = lax.map(window_fn, (tokens, key_proj, key_cot, gate_cot))
    grad_scale = float(SEQS * LEN) ** -0.5
    down_grad = jnp.sum(down_sum, axis=0) * grad_scale
    up_grad = jnp.sum(up_sum, axis=0) * grad_scale
    conv_grad = jnp.sum(conv_sum, axis=0) * grad_scale
    bias_grad = jnp.sum(bias_sum, axis=0) * grad_scale
    return input_grad, down_grad, up_grad, conv_grad, bias_grad
```

```python
import functools

import jax
import jax.numpy as jnp
from jax import lax
from jax.experimental import pallas as pl
from jax.experimental.pallas import tpu as pltpu
from jax.sharding import Mesh
from jax.sharding import PartitionSpec as P

CONV = 4
BF16 = jnp.bfloat16
F32 = jnp.float32
LANES = 128
SP = ("xl", "zh", "zl")
PLANE = ("fsdp", "xl", "dp")
VMEM = 16 * 2**20
PADDED = 48


def key_kernel(
    cot_ref, key_ref, before_ref, taps_ref, tokens_ref, part0, part1, part2, part3, bias_ref, up_ref,
    slope_ref, send_ref, latent_ref, ext_ref, down_ref,
):
    step = pl.program_id(0)
    blocks, rows, _ = cot_ref.shape
    ups = up_ref.shape[1]

    @pl.when(step == 0)
    def _():
        latent_grad = sum(part[...].astype(F32) for part in (part0, part1, part2, part3)).astype(BF16)
        latent_ref[...] = latent_grad
        down_ref[...] = lax.dot_general(
            tokens_ref[...], latent_grad, (((0,), (0,)), ((), ())), preferred_element_type=F32
        )

    taps = taps_ref[...].astype(F32)
    ext_ref[:8, :] = before_ref[...].astype(F32)
    ext_ref[8:, :] = key_ref[...].astype(F32)
    share = down_ref.shape[0] // (blocks * pl.num_programs(0))
    own = blocks * share
    down = down_ref[pl.ds(pl.multiple_of(step * own, 8), own), :]
    for block in range(blocks):
        cols = slice(block * LANES, (block + 1) * LANES)
        shifted_keys = [ext_ref[8 - j : 8 - j + rows, cols] for j in range(CONV)]
        conv_out = sum(taps[j : j + 1, cols] * shifted_keys[j] for j in range(CONV))
        squashed = jax.nn.sigmoid(conv_out)
        slope = squashed * (1.0 + conv_out * (1.0 - squashed))
        grad = (cot_ref[block].astype(F32) * slope).astype(BF16)
        slope_ref[:, cols] = grad
        grad = grad.astype(F32)
        terms = [down[block * share : (block + 1) * share]]
        terms += [jnp.sum(grad * shifted_keys[j], axis=0, keepdims=True) for j in range(CONV)]
        terms += [bias_ref[block], jnp.zeros((PADDED - share - CONV - 1, LANES), F32)]
        send_ref[block, :ups, :] = up_ref[block]
        send_ref[block, ups:, :] = jnp.concatenate(terms, axis=0).astype(BF16)


def key_stage(cot, keys, before, taps, tokens, parts, bias, ups):
    heads, rows, _ = cot.shape
    step = 4
    wide = step * LANES
    ups_rows = ups.shape[1]
    whole = lambda array: pl.BlockSpec(array.shape, lambda i: (0, 0))
    return pl.pallas_call(
        key_kernel,
        grid=(heads // step,),
        in_specs=[
            pl.BlockSpec((step, rows, LANES), lambda i: (i, 0, 0)),
            pl.BlockSpec((rows, wide), lambda i: (0, i)),
            pl.BlockSpec((8, wide), lambda i: (0, i)),
            pl.BlockSpec((CONV, wide), lambda i: (0, i)),
            whole(tokens),
            *(whole(part) for part in parts),
            pl.BlockSpec((step, 1, LANES), lambda i: (i, 0, 0)),
            pl.BlockSpec((step, ups_rows, LANES), lambda i: (i, 0, 0)),
        ],
        out_specs=[
            pl.BlockSpec((rows, wide), lambda i: (0, i)),
            pl.BlockSpec((step, ups_rows + PADDED, LANES), lambda i: (i, 0, 0)),
            whole(parts[0]),
        ],
        out_shape=[
            jax.ShapeDtypeStruct((rows, heads * LANES), BF16),
            jax.ShapeDtypeStruct((heads, ups_rows + PADDED, LANES), BF16),
            jax.ShapeDtypeStruct(parts[0].shape, BF16),
        ],
        scratch_shapes=[
            pltpu.VMEM((rows + 8, wide), F32),
            pltpu.VMEM((tokens.shape[1], LANES), F32),
        ],
        compiler_params=pltpu.CompilerParams(vmem_limit_bytes=VMEM),
        cost_estimate=pl.CostEstimate(
            flops=40 * heads * rows * LANES, bytes_accessed=3 * 2**20, transcendentals=heads * rows * LANES
        ),
        name="key_stage",
    )(cot, keys, before, taps, tokens, *parts, bias, ups)


def gate_kernel(
    at_ref, cot_ref, lat_ref, up_ref, bias_ref,
    part0, part1, part2, part3, send_ref, bias_out, sum_ref, grad_ref,
):
    zh = at_ref[0]
    rows = part0.shape[0]
    latent = lat_ref[...]
    ups = []
    for head in range(8):
        up_head = jnp.concatenate([up_ref[f, head] for f in range(8)], axis=0)
        ups.append(up_head)
        logits = jnp.dot(latent, up_head, preferred_element_type=F32) + bias_ref[head : head + 1, :]
        grad = (-cot_ref[head].astype(F32) * jax.nn.sigmoid(logits)).astype(BF16)
        grad_ref[head] = grad
        bias_out[head : head + 1, :] = jnp.sum(grad.astype(F32), axis=0, keepdims=True)
    partial = None
    for head in range(8):
        term = lax.dot_general(
            grad_ref[head], ups[head], (((1,), (1,)), ((), ())), preferred_element_type=F32
        )
        partial = term if partial is None else partial + term
    sum_ref[...] = partial.astype(BF16)
    for k, part in enumerate((part0, part1, part2, part3)):
        owner = lax.rem(zh + k, 4)
        part[...] = sum_ref[pl.ds(pl.multiple_of(owner * rows, rows), rows), :]
    for x in range(2):
        terms = [
            lax.dot_general(
                latent, grad_ref[x * 4 + zl], (((0,), (0,)), ((), ())), preferred_element_type=F32
            )
            for zl in range(4)
        ]
        for f in range(8):
            for dp in range(2):
                first = (f * 2 + dp) * 8
                send_ref[f * 4 + x * 2 + dp] = jnp.concatenate(
                    [term[first : first + 8] for term in terms], axis=0
                ).astype(BF16)


def gate_stage(at, cot, lat, up_rows, bias):
    tall, rank = lat.shape
    rows = tall // 4
    whole = pl.BlockSpec(memory_space=pltpu.VMEM)
    part = jax.ShapeDtypeStruct((rows, rank), BF16)
    return pl.pallas_call(
        gate_kernel,
        in_specs=[pl.BlockSpec(memory_space=pltpu.SMEM)] + [whole] * 4,
        out_specs=[whole] * 6,
        out_shape=[part] * 4
        + [jax.ShapeDtypeStruct((32, 32, LANES), BF16), jax.ShapeDtypeStruct((8, LANES), F32)],
        scratch_shapes=[pltpu.VMEM((tall, rank), BF16), pltpu.VMEM((8, tall, LANES), BF16)],
        compiler_params=pltpu.CompilerParams(vmem_limit_bytes=VMEM),
        cost_estimate=pl.CostEstimate(
            flops=6 * 8 * tall * rank * LANES, bytes_accessed=3 * 2**20, transcendentals=8 * tall * LANES
        ),
        name="gate_stage",
    )(at, cot, lat, up_rows, bias)


def input_kernel(slope_ref, after_ref, taps_ref, key_ref, latent_ref, down_ref, out_ref, sum_ref, ext_ref):
    step = pl.program_id(0)
    rows = slope_ref.shape[0]
    contract = (((1,), (1,)), ((), ()))

    @pl.when(step == 0)
    def _():
        sum_ref[...] = lax.dot_general(
            latent_ref[...], down_ref[...], contract, preferred_element_type=F32
        )

    taps = taps_ref[...].astype(F32)
    ext_ref[:rows, :] = slope_ref[...].astype(F32)
    ext_ref[rows:, :] = after_ref[...].astype(F32)
    grad = sum(taps[j : j + 1, :] * ext_ref[j : j + rows, :] for j in range(CONV)).astype(BF16)
    sum_ref[...] += lax.dot_general(grad, key_ref[...], contract, preferred_element_type=F32)

    @pl.when(step == pl.num_programs(0) - 1)
    def _():
        out_ref[...] = sum_ref[...].astype(BF16)


def input_stage(slope, after, taps, key_full, latent_grad, down_full):
    rows, channels = slope.shape
    width = key_full.shape[0]
    wide = 512
    return pl.pallas_call(
        input_kernel,
        grid=(channels // wide,),
        in_specs=[
            pl.BlockSpec((rows, wide), lambda i: (0, i)),
            pl.BlockSpec((8, wide), lambda i: (0, i)),
            pl.BlockSpec((CONV, wide), lambda i: (0, i)),
            pl.BlockSpec((width, wide), lambda i: (0, i)),
            pl.BlockSpec(latent_grad.shape, lambda i: (0, 0)),
            pl.BlockSpec(down_full.shape, lambda i: (0, 0)),
        ],
        out_specs=pl.BlockSpec((rows, width), lambda i: (0, 0)),
        out_shape=jax.ShapeDtypeStruct((rows, width), BF16),
        scratch_shapes=[pltpu.VMEM((rows, width), F32), pltpu.VMEM((rows + 8, wide), F32)],
        compiler_params=pltpu.CompilerParams(vmem_limit_bytes=VMEM),
        cost_estimate=pl.CostEstimate(
            flops=20 * 2 * rows * channels * width, bytes_accessed=80 * 2**20, transcendentals=0
        ),
        name="input_stage",
    )(slope, after, taps, key_full, latent_grad, down_full)


def finish_kernel(at_ref, shares_ref, down_ref, up_ref, conv_ref, bias_ref):
    xl = at_ref[0]
    shares, own_up = shares_ref.shape[0], up_ref.shape[0] // 2
    share = down_ref.shape[0] // shares
    for k in range(2):
        up_ref[k * own_up : (k + 1) * own_up, :] = shares_ref[2 * xl + k, :own_up, :]
    for i in range(shares):
        last = own_up + share
        down_ref[i * share : (i + 1) * share, :] = shares_ref[i, own_up:last, :]
        conv_ref[:, i * LANES : (i + 1) * LANES] = shares_ref[i, last : last + CONV, :]
        bias_ref[i : i + 1, :] = shares_ref[i, last + CONV : last + CONV + 1, :]


def finish_stage(at, shares, rows_down, rows_up):
    whole = pl.BlockSpec(memory_space=pltpu.VMEM)
    return pl.pallas_call(
        finish_kernel,
        in_specs=[pl.BlockSpec(memory_space=pltpu.SMEM), whole],
        out_specs=[whole] * 4,
        out_shape=[
            jax.ShapeDtypeStruct((rows_down, LANES), F32),
            jax.ShapeDtypeStruct((rows_up, LANES), F32),
            jax.ShapeDtypeStruct((CONV, shares.shape[0] * LANES), F32),
            jax.ShapeDtypeStruct((shares.shape[0], LANES), F32),
        ],
        compiler_params=pltpu.CompilerParams(vmem_limit_bytes=VMEM),
        name="finish_stage",
    )(at, shares)


def turned(block, axis, distance, size=4):
    return lax.ppermute(block, axis, [(i, (i + distance) % size) for i in range(size)])


def per_device(
    tokens, key_proj, key_cot, gate_cot, key_weight, gate_down, gate_up, gate_bias, conv_weight
):
    length = tokens.shape[1]
    count = 32
    rank = gate_down.shape[1]
    rows_down, rows_up = gate_down.shape[0], gate_up.shape[0]
    inputs, projected = tokens[0], key_proj[0]
    zh = lax.axis_index("zh")

    gate_blocks = gate_cot.reshape(2, 4, 4, length, LANES).transpose(0, 2, 1, 3, 4)
    gate_mid = lax.all_to_all(
        gate_blocks.reshape(8, 4 * length, LANES), ("xl", "zl"), 0, 0, tiled=True
    )
    before = lax.ppermute(projected[length - 8 :], SP, [(i, i + 1) for i in range(count - 1)])
    key_full = lax.all_gather(key_weight, "fsdp", axis=0, tiled=True)

    up_mine = lax.dynamic_index_in_dim(gate_up.reshape(rows_up, 2, 4, 4, LANES), zh, 2, False)
    up_mine = up_mine.reshape(rows_up, 8, LANES).transpose(1, 0, 2).reshape(8 * rows_up, LANES)
    factors = lax.all_gather(
        jnp.concatenate([gate_down, up_mine], axis=0), "fsdp", axis=0, tiled=False
    )
    down_full = factors[:, :rows_down].reshape(8 * rows_down, rank)
    up_rows = factors[:, rows_down:].reshape(8, 8, rows_up, LANES)
    latent = jnp.dot(inputs, down_full, preferred_element_type=F32).astype(BF16)
    lat_all = lax.all_gather(latent, "zh", axis=0, tiled=True)
    bias_mine = lax.dynamic_index_in_dim(gate_bias.reshape(2, 4, 4, LANES), zh, 1, False)
    *parts, up_send, bias_term = gate_stage(
        zh.astype(jnp.int32).reshape(1), gate_mid, lat_all, up_rows, bias_mine.reshape(8, LANES)
    )
    parts, key_cot = lax.optimization_barrier((parts, key_cot))
    key_seq = lax.all_to_all(key_cot.reshape(count, length, LANES), SP, 0, 0, tiled=True)
    parts = parts[:1] + [turned(parts[k], "zh", k) for k in range(1, 4)]
    bias_row = lax.dynamic_update_slice_in_dim(
        jnp.zeros((2, 4, 4, LANES), F32), bias_term.reshape(2, 1, 4, LANES), zh, 1
    ).reshape(count, 1, LANES)
    slope_grad, send, latent_grad = key_stage(
        key_seq, projected, before, conv_weight, inputs, parts, bias_row, up_send
    )

    following = lax.ppermute(slope_grad[:8], SP, [(i + 1, i) for i in range(count - 1)])
    plane = jnp.sum(lax.all_to_all(send, PLANE, 0, 0, tiled=True).astype(F32), axis=0)
    rows_share, own_up = rows_down // 4, rows_up // 2
    mixed = rows_share + CONV + 1
    same = (jnp.arange(4) == zh).reshape(4, 1, 1, 1)
    to_heads = jnp.where(same, plane[: 4 * own_up].reshape(1, 4, own_up, LANES), 0.0)
    to_all = jnp.broadcast_to(plane[4 * own_up : 4 * own_up + mixed], (4, 4, mixed, LANES))
    line = jnp.concatenate([to_heads, to_all], axis=2).astype(BF16)
    line = lax.all_to_all(
        line.reshape(16, own_up + mixed, LANES), ("zh", "zl"), 0, 0, tiled=True
    )
    input_grad = input_stage(
        slope_grad, following, conv_weight, key_full, latent_grad, down_full
    )[None]
    line, input_grad = lax.optimization_barrier((line, input_grad))
    done = jnp.sum(line.astype(F32), axis=0) * float(65536) ** (-0.5)
    shares = lax.all_to_all(
        jnp.broadcast_to(done[None], (4,) + done.shape), ("xl", "dp"), 0, 0, tiled=True
    )

    at = lax.axis_index("xl").astype(jnp.int32).reshape(1)
    down_own, up_own, conv_own, bias_own = finish_stage(at, shares, rows_down, rows_up)
    return input_grad, down_own, up_own, conv_own, bias_own.reshape(4 * LANES)


def solution(mesh):
    fine = Mesh(mesh.devices.reshape(2, 4, 4, 8, 2), ("xl", "zh", "zl", "fsdp", "dp"))
    windows = ("fsdp", "dp")
    return jax.shard_map(
        per_device,
        mesh=fine,
        in_specs=(
            P(windows, SP, None),
            P(windows, SP, None),
            P(windows, None, SP),
            P(windows, None, SP),
            P("fsdp", None),
            P("fsdp", None),
            P("fsdp", None),
            P(),
            P(),
        ),
        out_specs=(
            P(windows, SP, None),
            P("fsdp", None),
            P("fsdp", SP),
            P(None, "fsdp"),
            P("fsdp"),
        ),
        check_vma=False,
    )
```

```python
import functools

import jax
import jax.numpy as jnp
from jax import lax
from jax.experimental import pallas as pl
from jax.experimental.pallas import tpu as pltpu
from jax.sharding import Mesh
from jax.sharding import PartitionSpec as P

CONV = 4
BF16 = jnp.bfloat16
F32 = jnp.float32
LANES = 128
SP = ("xl", "zh", "zl")
PLANE = ("fsdp", "xl", "dp")
VMEM = 16 * 2**20
PADDED = 48


def key_kernel(cot_ref, key_ref, before_ref, taps_ref, slope_ref, conv_ref, ext_ref):
    blocks, rows, _ = cot_ref.shape
    taps = taps_ref[...].astype(F32)
    ext_ref[:8, :] = before_ref[...].astype(F32)
    ext_ref[8:, :] = key_ref[...].astype(F32)
    for block in range(blocks):
        cols = slice(block * LANES, (block + 1) * LANES)
        shifted_keys = [ext_ref[8 - j : 8 - j + rows, cols] for j in range(CONV)]
        conv_out = sum(taps[j : j + 1, cols] * shifted_keys[j] for j in range(CONV))
        squashed = jax.nn.sigmoid(conv_out)
        slope = squashed * (1.0 + conv_out * (1.0 - squashed))
        grad = (cot_ref[block].astype(F32) * slope).astype(BF16)
        slope_ref[:, cols] = grad
        grad = grad.astype(F32)
        conv_ref[block] = jnp.concatenate(
            [jnp.sum(grad * shifted_keys[j], axis=0, keepdims=True) for j in range(CONV)], axis=0
        )


def key_stage(cot, keys, before, taps):
    heads, rows, _ = cot.shape
    step = 4
    wide = step * LANES
    return pl.pallas_call(
        key_kernel,
        grid=(heads // step,),
        in_specs=[
            pl.BlockSpec((step, rows, LANES), lambda i: (i, 0, 0)),
            pl.BlockSpec((rows, wide), lambda i: (0, i)),
            pl.BlockSpec((8, wide), lambda i: (0, i)),
            pl.BlockSpec((CONV, wide), lambda i: (0, i)),
        ],
        out_specs=[
            pl.BlockSpec((rows, wide), lambda i: (0, i)),
            pl.BlockSpec((step, CONV, LANES), lambda i: (i, 0, 0)),
        ],
        out_shape=[
            jax.ShapeDtypeStruct((rows, heads * LANES), BF16),
            jax.ShapeDtypeStruct((heads, CONV, LANES), F32),
        ],
        scratch_shapes=[pltpu.VMEM((rows + 8, wide), F32)],
        compiler_params=pltpu.CompilerParams(vmem_limit_bytes=VMEM),
        cost_estimate=pl.CostEstimate(
            flops=40 * heads * rows * LANES, bytes_accessed=3 * 2**20, transcendentals=heads * rows * LANES
        ),
        name="key_stage",
    )(cot, keys, before, taps)


def pack_kernel(
    tokens_ref, part0, part1, part2, part3, conv_ref, bias_ref, up_ref, send_ref, latent_ref
):
    latent_grad = sum(part[...].astype(F32) for part in (part0, part1, part2, part3)).astype(BF16)
    latent_ref[...] = latent_grad
    down = lax.dot_general(
        tokens_ref[...], latent_grad, (((0,), (0,)), ((), ())), preferred_element_type=F32
    )
    peers, ups = up_ref.shape[0], up_ref.shape[1]
    share = down.shape[0] // peers
    rest = jnp.zeros((PADDED - share - CONV - 1, LANES), F32)
    for peer in range(peers):
        terms = [down[peer * share : (peer + 1) * share], conv_ref[peer], bias_ref[peer], rest]
        send_ref[peer, :ups, :] = up_ref[peer]
        send_ref[peer, ups:, :] = jnp.concatenate(terms, axis=0).astype(BF16)


def pack_stage(tokens, parts, conv, bias, ups):
    whole = pl.BlockSpec(memory_space=pltpu.VMEM)
    peers, ups_rows, _ = ups.shape
    return pl.pallas_call(
        pack_kernel,
        in_specs=[whole] * 8,
        out_specs=[whole] * 2,
        out_shape=[
            jax.ShapeDtypeStruct((peers, ups_rows + PADDED, LANES), BF16),
            jax.ShapeDtypeStruct(parts[0].shape, BF16),
        ],
        compiler_params=pltpu.CompilerParams(vmem_limit_bytes=VMEM),
        name="pack_stage",
    )(tokens, *parts, conv, bias, ups)


def gate_kernel(
    at_ref, cot_ref, lat_ref, up_ref, bias_ref,
    part0, part1, part2, part3, send_ref, bias_out, sum_ref, grad_ref,
):
    zh = at_ref[0]
    rows = part0.shape[0]
    latent = lat_ref[...]
    ups = []
    for head in range(8):
        up_head = jnp.concatenate([up_ref[f, head] for f in range(8)], axis=0)
        ups.append(up_head)
        logits = jnp.dot(latent, up_head, preferred_element_type=F32) + bias_ref[head : head + 1, :]
        grad = (-cot_ref[head].astype(F32) * jax.nn.sigmoid(logits)).astype(BF16)
        grad_ref[head] = grad
        bias_out[head : head + 1, :] = jnp.sum(grad.astype(F32), axis=0, keepdims=True)
    partial = None
    for head in range(8):
        term = lax.dot_general(
            grad_ref[head], ups[head], (((1,), (1,)), ((), ())), preferred_element_type=F32
        )
        partial = term if partial is None else partial + term
    sum_ref[...] = partial.astype(BF16)
    for k, part in enumerate((part0, part1, part2, part3)):
        owner = lax.rem(zh + k, 4)
        part[...] = sum_ref[pl.ds(pl.multiple_of(owner * rows, rows), rows), :]
    for x in range(2):
        terms = [
            lax.dot_general(
                latent, grad_ref[x * 4 + zl], (((0,), (0,)), ((), ())), preferred_element_type=F32
            )
            for zl in range(4)
        ]
        for f in range(8):
            for dp in range(2):
                first = (f * 2 + dp) * 8
                send_ref[f * 4 + x * 2 + dp] = jnp.concatenate(
                    [term[first : first + 8] for term in terms], axis=0
                ).astype(BF16)


def gate_stage(at, cot, lat, up_rows, bias):
    tall, rank = lat.shape
    rows = tall // 4
    whole = pl.BlockSpec(memory_space=pltpu.VMEM)
    part = jax.ShapeDtypeStruct((rows, rank), BF16)
    return pl.pallas_call(
        gate_kernel,
        in_specs=[pl.BlockSpec(memory_space=pltpu.SMEM)] + [whole] * 4,
        out_specs=[whole] * 6,
        out_shape=[part] * 4
        + [jax.ShapeDtypeStruct((32, 32, LANES), BF16), jax.ShapeDtypeStruct((8, LANES), F32)],
        scratch_shapes=[pltpu.VMEM((tall, rank), BF16), pltpu.VMEM((8, tall, LANES), BF16)],
        compiler_params=pltpu.CompilerParams(vmem_limit_bytes=VMEM),
        cost_estimate=pl.CostEstimate(
            flops=6 * 8 * tall * rank * LANES, bytes_accessed=3 * 2**20, transcendentals=8 * tall * LANES
        ),
        name="gate_stage",
    )(at, cot, lat, up_rows, bias)


def input_kernel(slope_ref, after_ref, taps_ref, key_ref, latent_ref, down_ref, out_ref, sum_ref, ext_ref):
    step = pl.program_id(0)
    rows = slope_ref.shape[0]
    contract = (((1,), (1,)), ((), ()))

    @pl.when(step == 0)
    def _():
        sum_ref[...] = lax.dot_general(
            latent_ref[...], down_ref[...], contract, preferred_element_type=F32
        )

    taps = taps_ref[...].astype(F32)
    ext_ref[:rows, :] = slope_ref[...].astype(F32)
    ext_ref[rows:, :] = after_ref[...].astype(F32)
    grad = sum(taps[j : j + 1, :] * ext_ref[j : j + rows, :] for j in range(CONV)).astype(BF16)
    sum_ref[...] += lax.dot_general(grad, key_ref[...], contract, preferred_element_type=F32)

    @pl.when(step == pl.num_programs(0) - 1)
    def _():
        out_ref[...] = sum_ref[...].astype(BF16)


def input_stage(slope, after, taps, key_full, latent_grad, down_full):
    rows, channels = slope.shape
    width = key_full.shape[0]
    wide = 512
    return pl.pallas_call(
        input_kernel,
        grid=(channels // wide,),
        in_specs=[
            pl.BlockSpec((rows, wide), lambda i: (0, i)),
            pl.BlockSpec((8, wide), lambda i: (0, i)),
            pl.BlockSpec((CONV, wide), lambda i: (0, i)),
            pl.BlockSpec((width, wide), lambda i: (0, i)),
            pl.BlockSpec(latent_grad.shape, lambda i: (0, 0)),
            pl.BlockSpec(down_full.shape, lambda i: (0, 0)),
        ],
        out_specs=pl.BlockSpec((rows, width), lambda i: (0, 0)),
        out_shape=jax.ShapeDtypeStruct((rows, width), BF16),
        scratch_shapes=[pltpu.VMEM((rows, width), F32), pltpu.VMEM((rows + 8, wide), F32)],
        compiler_params=pltpu.CompilerParams(vmem_limit_bytes=VMEM),
        cost_estimate=pl.CostEstimate(
            flops=20 * 2 * rows * channels * width, bytes_accessed=80 * 2**20, transcendentals=0
        ),
        name="input_stage",
    )(slope, after, taps, key_full, latent_grad, down_full)


def finish_kernel(at_ref, shares_ref, down_ref, up_ref, conv_ref, bias_ref):
    xl = at_ref[0]
    shares, own_up = shares_ref.shape[0], up_ref.shape[0] // 2
    share = down_ref.shape[0] // shares
    for k in range(2):
        up_ref[k * own_up : (k + 1) * own_up, :] = shares_ref[2 * xl + k, :own_up, :]
    for i in range(shares):
        last = own_up + share
        down_ref[i * share : (i + 1) * share, :] = shares_ref[i, own_up:last, :]
        conv_ref[:, i * LANES : (i + 1) * LANES] = shares_ref[i, last : last + CONV, :]
        bias_ref[i : i + 1, :] = shares_ref[i, last + CONV : last + CONV + 1, :]


def finish_stage(at, shares, rows_down, rows_up):
    whole = pl.BlockSpec(memory_space=pltpu.VMEM)
    return pl.pallas_call(
        finish_kernel,
        in_specs=[pl.BlockSpec(memory_space=pltpu.SMEM), whole],
        out_specs=[whole] * 4,
        out_shape=[
            jax.ShapeDtypeStruct((rows_down, LANES), F32),
            jax.ShapeDtypeStruct((rows_up, LANES), F32),
            jax.ShapeDtypeStruct((CONV, shares.shape[0] * LANES), F32),
            jax.ShapeDtypeStruct((shares.shape[0], LANES), F32),
        ],
        compiler_params=pltpu.CompilerParams(vmem_limit_bytes=VMEM),
        name="finish_stage",
    )(at, shares)


def turned(block, axis, distance, size=4):
    return lax.ppermute(block, axis, [(i, (i + distance) % size) for i in range(size)])


def per_device(
    tokens, key_proj, key_cot, gate_cot, key_weight, gate_down, gate_up, gate_bias, conv_weight
):
    length = tokens.shape[1]
    count = 32
    rank = gate_down.shape[1]
    rows_down, rows_up = gate_down.shape[0], gate_up.shape[0]
    inputs, projected = tokens[0], key_proj[0]
    zh = lax.axis_index("zh")

    gate_blocks = gate_cot.reshape(2, 4, 4, length, LANES).transpose(0, 2, 1, 3, 4)
    gate_mid = lax.all_to_all(
        gate_blocks.reshape(8, 4 * length, LANES), ("xl", "zl"), 0, 0, tiled=True
    )
    before = lax.ppermute(projected[length - 8 :], SP, [(i, i + 1) for i in range(count - 1)])
    key_full = lax.all_gather(key_weight, "fsdp", axis=0, tiled=True)

    up_mine = lax.dynamic_index_in_dim(gate_up.reshape(rows_up, 2, 4, 4, LANES), zh, 2, False)
    up_mine = up_mine.reshape(rows_up, 8, LANES).transpose(1, 0, 2).reshape(8 * rows_up, LANES)
    factors = lax.all_gather(
        jnp.concatenate([gate_down, up_mine], axis=0), "fsdp", axis=0, tiled=False
    )
    down_full = factors[:, :rows_down].reshape(8 * rows_down, rank)
    up_rows = factors[:, rows_down:].reshape(8, 8, rows_up, LANES)
    latent = jnp.dot(inputs, down_full, preferred_element_type=F32).astype(BF16)
    lat_all = lax.all_gather(latent, "zh", axis=0, tiled=True)
    bias_mine = lax.dynamic_index_in_dim(gate_bias.reshape(2, 4, 4, LANES), zh, 1, False)
    *parts, up_send, bias_term = gate_stage(
        zh.astype(jnp.int32).reshape(1), gate_mid, lat_all, up_rows, bias_mine.reshape(8, LANES)
    )
    parts, key_cot = lax.optimization_barrier((parts, key_cot))
    key_seq = lax.all_to_all(key_cot.reshape(count, length, LANES), SP, 0, 0, tiled=True)
    parts = parts[:1] + [turned(parts[k], "zh", k) for k in range(1, 4)]
    bias_row = lax.dynamic_update_slice_in_dim(
        jnp.zeros((2, 4, 4, LANES), F32), bias_term.reshape(2, 1, 4, LANES), zh, 1
    ).reshape(count, 1, LANES)
    slope_grad, conv_term = key_stage(key_seq, projected, before, conv_weight)
    parts, conv_term = lax.optimization_barrier((parts, conv_term))
    send, latent_grad = pack_stage(inputs, parts, conv_term, bias_row, up_send)

    following = lax.ppermute(slope_grad[:8], SP, [(i + 1, i) for i in range(count - 1)])
    plane = jnp.sum(lax.all_to_all(send, PLANE, 0, 0, tiled=True).astype(F32), axis=0)
    rows_share, own_up = rows_down // 4, rows_up // 2
    mixed = rows_share + CONV + 1
    same = (jnp.arange(4) == zh).reshape(4, 1, 1, 1)
    to_heads = jnp.where(same, plane[: 4 * own_up].reshape(1, 4, own_up, LANES), 0.0)
    to_all = jnp.broadcast_to(plane[4 * own_up : 4 * own_up + mixed], (4, 4, mixed, LANES))
    line = jnp.concatenate([to_heads, to_all], axis=2).astype(BF16)
    line = lax.all_to_all(
        line.reshape(16, own_up + mixed, LANES), ("zh", "zl"), 0, 0, tiled=True
    )
    input_grad = input_stage(
        slope_grad, following, conv_weight, key_full, latent_grad, down_full
    )[None]
    line, input_grad = lax.optimization_barrier((line, input_grad))
    done = jnp.sum(line.astype(F32), axis=0) * float(65536) ** (-0.5)
    shares = lax.all_to_all(
        jnp.broadcast_to(done[None], (4,) + done.shape), ("xl", "dp"), 0, 0, tiled=True
    )

    at = lax.axis_index("xl").astype(jnp.int32).reshape(1)
    down_own, up_own, conv_own, bias_own = finish_stage(at, shares, rows_down, rows_up)
    return input_grad, down_own, up_own, conv_own, bias_own.reshape(4 * LANES)


def solution(mesh):
    fine = Mesh(mesh.devices.reshape(2, 4, 4, 8, 2), ("xl", "zh", "zl", "fsdp", "dp"))
    windows = ("fsdp", "dp")
    return jax.shard_map(
        per_device,
        mesh=fine,
        in_specs=(
            P(windows, SP, None),
            P(windows, SP, None),
            P(windows, None, SP),
            P(windows, None, SP),
            P("fsdp", None),
            P("fsdp", None),
            P("fsdp", None),
            P(),
            P(),
        ),
        out_specs=(
            P(windows, SP, None),
            P("fsdp", None),
            P("fsdp", SP),
            P(None, "fsdp"),
            P("fsdp"),
        ),
        check_vma=False,
    )
```

```python
import functools

import jax
import jax.numpy as jnp
from jax import lax
from jax.experimental import pallas as pl
from jax.experimental.pallas import tpu as pltpu
from jax.sharding import Mesh
from jax.sharding import PartitionSpec as P

CONV = 4
BF16 = jnp.bfloat16
F32 = jnp.float32
LANES = 128
SP = ("xl", "zh", "zl")
PLANE = ("fsdp", "xl", "dp")
VMEM = 16 * 2**20
PADDED = 48


def key_kernel(cot_ref, key_ref, before_ref, taps_ref, slope_ref, conv_ref, ext_ref):
    blocks, rows, _ = cot_ref.shape
    taps = taps_ref[...].astype(F32)
    ext_ref[:8, :] = before_ref[...].astype(F32)
    ext_ref[8:, :] = key_ref[...].astype(F32)
    for block in range(blocks):
        cols = slice(block * LANES, (block + 1) * LANES)
        shifted_keys = [ext_ref[8 - j : 8 - j + rows, cols] for j in range(CONV)]
        conv_out = sum(taps[j : j + 1, cols] * shifted_keys[j] for j in range(CONV))
        squashed = jax.nn.sigmoid(conv_out)
        slope = squashed * (1.0 + conv_out * (1.0 - squashed))
        grad = (cot_ref[block].astype(F32) * slope).astype(BF16)
        slope_ref[:, cols] = grad
        grad = grad.astype(F32)
        conv_ref[block] = jnp.concatenate(
            [jnp.sum(grad * shifted_keys[j], axis=0, keepdims=True) for j in range(CONV)], axis=0
        )


def key_stage(cot, keys, before, taps):
    heads, rows, _ = cot.shape
    step = 4
    wide = step * LANES
    return pl.pallas_call(
        key_kernel,
        grid=(heads // step,),
        in_specs=[
            pl.BlockSpec((step, rows, LANES), lambda i: (i, 0, 0)),
            pl.BlockSpec((rows, wide), lambda i: (0, i)),
            pl.BlockSpec((8, wide), lambda i: (0, i)),
            pl.BlockSpec((CONV, wide), lambda i: (0, i)),
        ],
        out_specs=[
            pl.BlockSpec((rows, wide), lambda i: (0, i)),
            pl.BlockSpec((step, CONV, LANES), lambda i: (i, 0, 0)),
        ],
        out_shape=[
            jax.ShapeDtypeStruct((rows, heads * LANES), BF16),
            jax.ShapeDtypeStruct((heads, CONV, LANES), F32),
        ],
        scratch_shapes=[pltpu.VMEM((rows + 8, wide), F32)],
        compiler_params=pltpu.CompilerParams(vmem_limit_bytes=VMEM),
        cost_estimate=pl.CostEstimate(
            flops=40 * heads * rows * LANES, bytes_accessed=3 * 2**20, transcendentals=heads * rows * LANES
        ),
        name="key_stage",
    )(cot, keys, before, taps)


def pack_kernel(
    tokens_ref, part0, part1, part2, part3, conv_ref, bias_ref, up_ref, send_ref, latent_ref
):
    latent_grad = sum(part[...].astype(F32) for part in (part0, part1, part2, part3)).astype(BF16)
    latent_ref[...] = latent_grad
    down = lax.dot_general(
        tokens_ref[...], latent_grad, (((0,), (0,)), ((), ())), preferred_element_type=F32
    )
    peers, ups = up_ref.shape[0], up_ref.shape[1]
    share = down.shape[0] // peers
    rest = jnp.zeros((PADDED - share - CONV - 1, LANES), F32)
    for peer in range(peers):
        terms = [down[peer * share : (peer + 1) * share], conv_ref[peer], bias_ref[peer], rest]
        send_ref[peer, :ups, :] = up_ref[peer]
        send_ref[peer, ups:, :] = jnp.concatenate(terms, axis=0).astype(BF16)


def pack_stage(tokens, parts, conv, bias, ups):
    whole = pl.BlockSpec(memory_space=pltpu.VMEM)
    peers, ups_rows, _ = ups.shape
    return pl.pallas_call(
        pack_kernel,
        in_specs=[whole] * 8,
        out_specs=[whole] * 2,
        out_shape=[
            jax.ShapeDtypeStruct((peers, ups_rows + PADDED, LANES), BF16),
            jax.ShapeDtypeStruct(parts[0].shape, BF16),
        ],
        compiler_params=pltpu.CompilerParams(vmem_limit_bytes=VMEM),
        name="pack_stage",
    )(tokens, *parts, conv, bias, ups)


def gate_kernel(
    at_ref, cot_ref, lat_ref, up_ref, bias_ref,
    part0, part1, part2, part3, send_ref, bias_out, sum_ref, grad_ref,
):
    zh = at_ref[0]
    rows = part0.shape[0]
    latent = lat_ref[...]
    ups = []
    for head in range(8):
        up_head = jnp.concatenate([up_ref[f, head] for f in range(8)], axis=0)
        ups.append(up_head)
        logits = jnp.dot(latent, up_head, preferred_element_type=F32) + bias_ref[head : head + 1, :]
        grad = (-cot_ref[head].astype(F32) * jax.nn.sigmoid(logits)).astype(BF16)
        grad_ref[head] = grad
        bias_out[head : head + 1, :] = jnp.sum(grad.astype(F32), axis=0, keepdims=True)
    partial = None
    for head in range(8):
        term = lax.dot_general(
            grad_ref[head], ups[head], (((1,), (1,)), ((), ())), preferred_element_type=F32
        )
        partial = term if partial is None else partial + term
    sum_ref[...] = partial.astype(BF16)
    for k, part in enumerate((part0, part1, part2, part3)):
        owner = lax.rem(zh + k, 4)
        part[...] = sum_ref[pl.ds(pl.multiple_of(owner * rows, rows), rows), :]
    for x in range(2):
        terms = [
            lax.dot_general(
                latent, grad_ref[x * 4 + zl], (((0,), (0,)), ((), ())), preferred_element_type=F32
            )
            for zl in range(4)
        ]
        for f in range(8):
            for dp in range(2):
                first = (f * 2 + dp) * 8
                send_ref[f * 4 + x * 2 + dp] = jnp.concatenate(
                    [term[first : first + 8] for term in terms], axis=0
                ).astype(BF16)


def gate_stage(at, cot, lat, up_rows, bias):
    tall, rank = lat.shape
    rows = tall // 4
    whole = pl.BlockSpec(memory_space=pltpu.VMEM)
    part = jax.ShapeDtypeStruct((rows, rank), BF16)
    return pl.pallas_call(
        gate_kernel,
        in_specs=[pl.BlockSpec(memory_space=pltpu.SMEM)] + [whole] * 4,
        out_specs=[whole] * 6,
        out_shape=[part] * 4
        + [jax.ShapeDtypeStruct((32, 32, LANES), BF16), jax.ShapeDtypeStruct((8, LANES), F32)],
        scratch_shapes=[pltpu.VMEM((tall, rank), BF16), pltpu.VMEM((8, tall, LANES), BF16)],
        compiler_params=pltpu.CompilerParams(vmem_limit_bytes=VMEM),
        cost_estimate=pl.CostEstimate(
            flops=6 * 8 * tall * rank * LANES, bytes_accessed=3 * 2**20, transcendentals=8 * tall * LANES
        ),
        name="gate_stage",
    )(at, cot, lat, up_rows, bias)


def input_kernel(slope_ref, after_ref, taps_ref, key_ref, latent_ref, down_ref, out_ref, sum_ref, ext_ref):
    step = pl.program_id(0)
    rows = slope_ref.shape[0]
    contract = (((1,), (1,)), ((), ()))

    @pl.when(step == 0)
    def _():
        sum_ref[...] = lax.dot_general(
            latent_ref[...], down_ref[...], contract, preferred_element_type=F32
        )

    taps = taps_ref[...].astype(F32)
    ext_ref[:rows, :] = slope_ref[...].astype(F32)
    ext_ref[rows:, :] = after_ref[...].astype(F32)
    grad = sum(taps[j : j + 1, :] * ext_ref[j : j + rows, :] for j in range(CONV)).astype(BF16)
    sum_ref[...] += lax.dot_general(grad, key_ref[...], contract, preferred_element_type=F32)

    @pl.when(step == pl.num_programs(0) - 1)
    def _():
        out_ref[...] = sum_ref[...].astype(BF16)


def input_stage(slope, after, taps, key_full, latent_grad, down_full):
    rows, channels = slope.shape
    width = key_full.shape[0]
    wide = 512
    return pl.pallas_call(
        input_kernel,
        grid=(channels // wide,),
        in_specs=[
            pl.BlockSpec((rows, wide), lambda i: (0, i)),
            pl.BlockSpec((8, wide), lambda i: (0, i)),
            pl.BlockSpec((CONV, wide), lambda i: (0, i)),
            pl.BlockSpec((width, wide), lambda i: (0, i)),
            pl.BlockSpec(latent_grad.shape, lambda i: (0, 0)),
            pl.BlockSpec(down_full.shape, lambda i: (0, 0)),
        ],
        out_specs=pl.BlockSpec((rows, width), lambda i: (0, 0)),
        out_shape=jax.ShapeDtypeStruct((rows, width), BF16),
        scratch_shapes=[pltpu.VMEM((rows, width), F32), pltpu.VMEM((rows + 8, wide), F32)],
        compiler_params=pltpu.CompilerParams(vmem_limit_bytes=VMEM),
        cost_estimate=pl.CostEstimate(
            flops=20 * 2 * rows * channels * width, bytes_accessed=80 * 2**20, transcendentals=0
        ),
        name="input_stage",
    )(slope, after, taps, key_full, latent_grad, down_full)


def finish_kernel(at_ref, shares_ref, down_ref, up_ref, conv_ref, bias_ref):
    xl = at_ref[0]
    shares, own_up = shares_ref.shape[0], up_ref.shape[0] // 2
    share = down_ref.shape[0] // shares
    for k in range(2):
        up_ref[k * own_up : (k + 1) * own_up, :] = shares_ref[2 * xl + k, :own_up, :]
    for i in range(shares):
        last = own_up + share
        down_ref[i * share : (i + 1) * share, :] = shares_ref[i, own_up:last, :]
        conv_ref[:, i * LANES : (i + 1) * LANES] = shares_ref[i, last : last + CONV, :]
        bias_ref[i : i + 1, :] = shares_ref[i, last + CONV : last + CONV + 1, :]


def finish_stage(at, shares, rows_down, rows_up):
    whole = pl.BlockSpec(memory_space=pltpu.VMEM)
    return pl.pallas_call(
        finish_kernel,
        in_specs=[pl.BlockSpec(memory_space=pltpu.SMEM), whole],
        out_specs=[whole] * 4,
        out_shape=[
            jax.ShapeDtypeStruct((rows_down, LANES), F32),
            jax.ShapeDtypeStruct((rows_up, LANES), F32),
            jax.ShapeDtypeStruct((CONV, shares.shape[0] * LANES), F32),
            jax.ShapeDtypeStruct((shares.shape[0], LANES), F32),
        ],
        compiler_params=pltpu.CompilerParams(vmem_limit_bytes=VMEM),
        name="finish_stage",
    )(at, shares)


def turned(block, axis, distance, size=4):
    return lax.ppermute(block, axis, [(i, (i + distance) % size) for i in range(size)])


def per_device(
    tokens, key_proj, key_cot, gate_cot, key_weight, gate_down, gate_up, gate_bias, conv_weight
):
    length = tokens.shape[1]
    count = 32
    rank = gate_down.shape[1]
    rows_down, rows_up = gate_down.shape[0], gate_up.shape[0]
    inputs, projected = tokens[0], key_proj[0]
    zh = lax.axis_index("zh")

    gate_blocks = gate_cot.reshape(2, 4, 4, length, LANES).transpose(0, 2, 1, 3, 4)
    gate_mid = lax.all_to_all(
        gate_blocks.reshape(8, 4 * length, LANES), ("xl", "zl"), 0, 0, tiled=True
    )
    before = lax.ppermute(projected[length - 8 :], SP, [(i, i + 1) for i in range(count - 1)])
    key_full = lax.all_gather(key_weight, "fsdp", axis=0, tiled=True)

    up_mine = lax.dynamic_index_in_dim(gate_up.reshape(rows_up, 2, 4, 4, LANES), zh, 2, False)
    up_mine = up_mine.reshape(rows_up, 8, LANES).transpose(1, 0, 2).reshape(8 * rows_up, LANES)
    factors = lax.all_gather(
        jnp.concatenate([gate_down, up_mine], axis=0), "fsdp", axis=0, tiled=False
    )
    down_full = factors[:, :rows_down].reshape(8 * rows_down, rank)
    up_rows = factors[:, rows_down:].reshape(8, 8, rows_up, LANES)
    latent = jnp.dot(inputs, down_full, preferred_element_type=F32).astype(BF16)
    lat_all = lax.all_gather(latent, "zh", axis=0, tiled=True)
    lat_all, key_cot = lax.optimization_barrier((lat_all, key_cot))
    key_seq = lax.all_to_all(key_cot.reshape(count, length, LANES), SP, 0, 0, tiled=True)
    bias_mine = lax.dynamic_index_in_dim(gate_bias.reshape(2, 4, 4, LANES), zh, 1, False)
    *parts, up_send, bias_term = gate_stage(
        zh.astype(jnp.int32).reshape(1), gate_mid, lat_all, up_rows, bias_mine.reshape(8, LANES)
    )
    far, ahead, behind = (turned(parts[k], "zh", k) for k in (2, 1, 3))
    parts = [parts[0], ahead, far, behind]
    bias_row = lax.dynamic_update_slice_in_dim(
        jnp.zeros((2, 4, 4, LANES), F32), bias_term.reshape(2, 1, 4, LANES), zh, 1
    ).reshape(count, 1, LANES)
    slope_grad, conv_term = key_stage(key_seq, projected, before, conv_weight)
    parts, conv_term = lax.optimization_barrier((parts, conv_term))
    send, latent_grad = pack_stage(inputs, parts, conv_term, bias_row, up_send)

    following = lax.ppermute(slope_grad[:8], SP, [(i + 1, i) for i in range(count - 1)])
    plane = jnp.sum(lax.all_to_all(send, PLANE, 0, 0, tiled=True).astype(F32), axis=0)
    rows_share, own_up = rows_down // 4, rows_up // 2
    mixed = rows_share + CONV + 1
    same = (jnp.arange(4) == zh).reshape(4, 1, 1, 1)
    to_heads = jnp.where(same, plane[: 4 * own_up].reshape(1, 4, own_up, LANES), 0.0)
    to_all = jnp.broadcast_to(plane[4 * own_up : 4 * own_up + mixed], (4, 4, mixed, LANES))
    line = jnp.concatenate([to_heads, to_all], axis=2).astype(BF16)
    line = lax.all_to_all(
        line.reshape(16, own_up + mixed, LANES), ("zh", "zl"), 0, 0, tiled=True
    )
    input_grad = input_stage(
        slope_grad, following, conv_weight, key_full, latent_grad, down_full
    )[None]
    line, input_grad = lax.optimization_barrier((line, input_grad))
    done = jnp.sum(line.astype(F32), axis=0) * float(65536) ** (-0.5)
    shares = lax.all_to_all(
        jnp.broadcast_to(done[None], (4,) + done.shape), ("xl", "dp"), 0, 0, tiled=True
    )

    at = lax.axis_index("xl").astype(jnp.int32).reshape(1)
    down_own, up_own, conv_own, bias_own = finish_stage(at, shares, rows_down, rows_up)
    return input_grad, down_own, up_own, conv_own, bias_own.reshape(4 * LANES)


def solution(mesh):
    fine = Mesh(mesh.devices.reshape(2, 4, 4, 8, 2), ("xl", "zh", "zl", "fsdp", "dp"))
    windows = ("fsdp", "dp")
    return jax.shard_map(
        per_device,
        mesh=fine,
        in_specs=(
            P(windows, SP, None),
            P(windows, SP, None),
            P(windows, None, SP),
            P(windows, None, SP),
            P("fsdp", None),
            P("fsdp", None),
            P("fsdp", None),
            P(),
            P(),
        ),
        out_specs=(
            P(windows, SP, None),
            P("fsdp", None),
            P("fsdp", SP),
            P(None, "fsdp"),
            P("fsdp"),
        ),
        check_vma=False,
    )
```

```python
import functools

import jax
import jax.numpy as jnp
from jax import lax
from jax.experimental import pallas as pl
from jax.experimental.pallas import tpu as pltpu
from jax.sharding import Mesh
from jax.sharding import PartitionSpec as P

CONV = 4
BF16 = jnp.bfloat16
F32 = jnp.float32
LANES = 128
SP = ("xl", "zh", "zl")
PLANE = ("fsdp", "xl", "dp")
VMEM = 16 * 2**20
PADDED = 48


def key_kernel(cot_ref, key_ref, before_ref, taps_ref, slope_ref, conv_ref, ext_ref):
    blocks, rows, _ = cot_ref.shape
    taps = taps_ref[...].astype(F32)
    ext_ref[:8, :] = before_ref[...].astype(F32)
    ext_ref[8:, :] = key_ref[...].astype(F32)
    for block in range(blocks):
        cols = slice(block * LANES, (block + 1) * LANES)
        shifted_keys = [ext_ref[8 - j : 8 - j + rows, cols] for j in range(CONV)]
        conv_out = sum(taps[j : j + 1, cols] * shifted_keys[j] for j in range(CONV))
        squashed = jax.nn.sigmoid(conv_out)
        slope = squashed * (1.0 + conv_out * (1.0 - squashed))
        grad = (cot_ref[block].astype(F32) * slope).astype(BF16)
        slope_ref[:, cols] = grad
        grad = grad.astype(F32)
        conv_ref[block] = jnp.concatenate(
            [jnp.sum(grad * shifted_keys[j], axis=0, keepdims=True) for j in range(CONV)], axis=0
        )


def key_stage(cot, keys, before, taps):
    heads, rows, _ = cot.shape
    step = 4
    wide = step * LANES
    return pl.pallas_call(
        key_kernel,
        grid=(heads // step,),
        in_specs=[
            pl.BlockSpec((step, rows, LANES), lambda i: (i, 0, 0)),
            pl.BlockSpec((rows, wide), lambda i: (0, i)),
            pl.BlockSpec((8, wide), lambda i: (0, i)),
            pl.BlockSpec((CONV, wide), lambda i: (0, i)),
        ],
        out_specs=[
            pl.BlockSpec((rows, wide), lambda i: (0, i)),
            pl.BlockSpec((step, CONV, LANES), lambda i: (i, 0, 0)),
        ],
        out_shape=[
            jax.ShapeDtypeStruct((rows, heads * LANES), BF16),
            jax.ShapeDtypeStruct((heads, CONV, LANES), F32),
        ],
        scratch_shapes=[pltpu.VMEM((rows + 8, wide), F32)],
        compiler_params=pltpu.CompilerParams(vmem_limit_bytes=VMEM),
        cost_estimate=pl.CostEstimate(
            flops=40 * heads * rows * LANES, bytes_accessed=3 * 2**20, transcendentals=heads * rows * LANES
        ),
        name="key_stage",
    )(cot, keys, before, taps)


def pack_kernel(
    tokens_ref, part0, part1, part2, part3, conv_ref, bias_ref, up_ref, send_ref, latent_ref
):
    latent_grad = sum(part[...].astype(F32) for part in (part0, part1, part2, part3)).astype(BF16)
    latent_ref[...] = latent_grad
    down = lax.dot_general(
        tokens_ref[...], latent_grad, (((0,), (0,)), ((), ())), preferred_element_type=F32
    )
    peers, ups = up_ref.shape[0], up_ref.shape[1]
    share = down.shape[0] // peers
    rest = jnp.zeros((PADDED - share - CONV - 1, LANES), F32)
    for peer in range(peers):
        terms = [down[peer * share : (peer + 1) * share], conv_ref[peer], bias_ref[peer], rest]
        send_ref[peer, :ups, :] = up_ref[peer]
        send_ref[peer, ups:, :] = jnp.concatenate(terms, axis=0).astype(BF16)


def pack_stage(tokens, parts, conv, bias, ups):
    whole = pl.BlockSpec(memory_space=pltpu.VMEM)
    peers, ups_rows, _ = ups.shape
    return pl.pallas_call(
        pack_kernel,
        in_specs=[whole] * 8,
        out_specs=[whole] * 2,
        out_shape=[
            jax.ShapeDtypeStruct((peers, ups_rows + PADDED, LANES), BF16),
            jax.ShapeDtypeStruct(parts[0].shape, BF16),
        ],
        compiler_params=pltpu.CompilerParams(vmem_limit_bytes=VMEM),
        name="pack_stage",
    )(tokens, *parts, conv, bias, ups)


def gate_kernel(
    at_ref, cot_ref, lat_ref, up_ref, bias_ref,
    part0, part1, part2, part3, send_ref, bias_out, sum_ref, grad_ref,
):
    zh = at_ref[0]
    rows = part0.shape[0]
    latent = lat_ref[...]
    ups = []
    for head in range(8):
        up_head = jnp.concatenate([up_ref[f, head] for f in range(8)], axis=0)
        ups.append(up_head)
        logits = jnp.dot(latent, up_head, preferred_element_type=F32) + bias_ref[head : head + 1, :]
        grad = (-cot_ref[head].astype(F32) * jax.nn.sigmoid(logits)).astype(BF16)
        grad_ref[head] = grad
        bias_out[head : head + 1, :] = jnp.sum(grad.astype(F32), axis=0, keepdims=True)
    partial = None
    for head in range(8):
        term = lax.dot_general(
            grad_ref[head], ups[head], (((1,), (1,)), ((), ())), preferred_element_type=F32
        )
        partial = term if partial is None else partial + term
    sum_ref[...] = partial.astype(BF16)
    for k, part in enumerate((part0, part1, part2, part3)):
        owner = lax.rem(zh + k, 4)
        part[...] = sum_ref[pl.ds(pl.multiple_of(owner * rows, rows), rows), :]
    for x in range(2):
        terms = [
            lax.dot_general(
                latent, grad_ref[x * 4 + zl], (((0,), (0,)), ((), ())), preferred_element_type=F32
            )
            for zl in range(4)
        ]
        for f in range(8):
            for dp in range(2):
                first = (f * 2 + dp) * 8
                send_ref[f * 4 + x * 2 + dp] = jnp.concatenate(
                    [term[first : first + 8] for term in terms], axis=0
                ).astype(BF16)


def gate_stage(at, cot, lat, up_rows, bias):
    tall, rank = lat.shape
    rows = tall // 4
    whole = pl.BlockSpec(memory_space=pltpu.VMEM)
    part = jax.ShapeDtypeStruct((rows, rank), BF16)
    return pl.pallas_call(
        gate_kernel,
        in_specs=[pl.BlockSpec(memory_space=pltpu.SMEM)] + [whole] * 4,
        out_specs=[whole] * 6,
        out_shape=[part] * 4
        + [jax.ShapeDtypeStruct((32, 32, LANES), BF16), jax.ShapeDtypeStruct((8, LANES), F32)],
        scratch_shapes=[pltpu.VMEM((tall, rank), BF16), pltpu.VMEM((8, tall, LANES), BF16)],
        compiler_params=pltpu.CompilerParams(vmem_limit_bytes=VMEM),
        cost_estimate=pl.CostEstimate(
            flops=6 * 8 * tall * rank * LANES, bytes_accessed=3 * 2**20, transcendentals=8 * tall * LANES
        ),
        name="gate_stage",
    )(at, cot, lat, up_rows, bias)


def input_kernel(slope_ref, after_ref, taps_ref, key_ref, latent_ref, down_ref, out_ref, sum_ref, ext_ref):
    step = pl.program_id(0)
    rows = slope_ref.shape[0]
    contract = (((1,), (1,)), ((), ()))

    @pl.when(step == 0)
    def _():
        sum_ref[...] = lax.dot_general(
            latent_ref[...], down_ref[...], contract, preferred_element_type=F32
        )

    taps = taps_ref[...].astype(F32)
    ext_ref[:rows, :] = slope_ref[...].astype(F32)
    ext_ref[rows:, :] = after_ref[...].astype(F32)
    grad = sum(taps[j : j + 1, :] * ext_ref[j : j + rows, :] for j in range(CONV)).astype(BF16)
    sum_ref[...] += lax.dot_general(grad, key_ref[...], contract, preferred_element_type=F32)

    @pl.when(step == pl.num_programs(0) - 1)
    def _():
        out_ref[...] = sum_ref[...].astype(BF16)


def input_stage(slope, after, taps, key_full, latent_grad, down_full):
    rows, channels = slope.shape
    width = key_full.shape[0]
    wide = 512
    return pl.pallas_call(
        input_kernel,
        grid=(channels // wide,),
        in_specs=[
            pl.BlockSpec((rows, wide), lambda i: (0, i)),
            pl.BlockSpec((8, wide), lambda i: (0, i)),
            pl.BlockSpec((CONV, wide), lambda i: (0, i)),
            pl.BlockSpec((width, wide), lambda i: (0, i)),
            pl.BlockSpec(latent_grad.shape, lambda i: (0, 0)),
            pl.BlockSpec(down_full.shape, lambda i: (0, 0)),
        ],
        out_specs=pl.BlockSpec((rows, width), lambda i: (0, 0)),
        out_shape=jax.ShapeDtypeStruct((rows, width), BF16),
        scratch_shapes=[pltpu.VMEM((rows, width), F32), pltpu.VMEM((rows + 8, wide), F32)],
        compiler_params=pltpu.CompilerParams(vmem_limit_bytes=VMEM),
        cost_estimate=pl.CostEstimate(
            flops=20 * 2 * rows * channels * width, bytes_accessed=80 * 2**20, transcendentals=0
        ),
        name="input_stage",
    )(slope, after, taps, key_full, latent_grad, down_full)


def finish_kernel(at_ref, shares_ref, down_ref, up_ref, conv_ref, bias_ref):
    xl = at_ref[0]
    shares, own_up = shares_ref.shape[0], up_ref.shape[0] // 2
    share = down_ref.shape[0] // shares
    for k in range(2):
        up_ref[k * own_up : (k + 1) * own_up, :] = shares_ref[2 * xl + k, :own_up, :]
    for i in range(shares):
        last = own_up + share
        down_ref[i * share : (i + 1) * share, :] = shares_ref[i, own_up:last, :]
        conv_ref[:, i * LANES : (i + 1) * LANES] = shares_ref[i, last : last + CONV, :]
        bias_ref[i : i + 1, :] = shares_ref[i, last + CONV : last + CONV + 1, :]


def finish_stage(at, shares, rows_down, rows_up):
    whole = pl.BlockSpec(memory_space=pltpu.VMEM)
    return pl.pallas_call(
        finish_kernel,
        in_specs=[pl.BlockSpec(memory_space=pltpu.SMEM), whole],
        out_specs=[whole] * 4,
        out_shape=[
            jax.ShapeDtypeStruct((rows_down, LANES), F32),
            jax.ShapeDtypeStruct((rows_up, LANES), F32),
            jax.ShapeDtypeStruct((CONV, shares.shape[0] * LANES), F32),
            jax.ShapeDtypeStruct((shares.shape[0], LANES), F32),
        ],
        compiler_params=pltpu.CompilerParams(vmem_limit_bytes=VMEM),
        name="finish_stage",
    )(at, shares)


def turned(block, axis, distance, size=4):
    return lax.ppermute(block, axis, [(i, (i + distance) % size) for i in range(size)])


def per_device(
    tokens, key_proj, key_cot, gate_cot, key_weight, gate_down, gate_up, gate_bias, conv_weight
):
    length = tokens.shape[1]
    count = 32
    rank = gate_down.shape[1]
    rows_down, rows_up = gate_down.shape[0], gate_up.shape[0]
    inputs, projected = tokens[0], key_proj[0]
    zh = lax.axis_index("zh")

    gate_blocks = gate_cot.reshape(2, 4, 4, length, LANES).transpose(0, 2, 1, 3, 4)
    gate_mid = lax.all_to_all(
        gate_blocks.reshape(8, 4 * length, LANES), ("xl", "zl"), 0, 0, tiled=True
    )
    before = lax.ppermute(projected[length - 8 :], SP, [(i, i + 1) for i in range(count - 1)])
    key_full = lax.all_gather(key_weight, "fsdp", axis=0, tiled=True)

    up_mine = lax.dynamic_index_in_dim(gate_up.reshape(rows_up, 2, 4, 4, LANES), zh, 2, False)
    up_mine = up_mine.reshape(rows_up, 8, LANES).transpose(1, 0, 2).reshape(8 * rows_up, LANES)
    factors = lax.all_gather(
        jnp.concatenate([gate_down, up_mine], axis=0), "fsdp", axis=0, tiled=False
    )
    down_full = factors[:, :rows_down].reshape(8 * rows_down, rank)
    up_rows = factors[:, rows_down:].reshape(8, 8, rows_up, LANES)
    latent = jnp.dot(inputs, down_full, preferred_element_type=F32).astype(BF16)
    lat_all = lax.all_gather(latent, "zh", axis=0, tiled=True)
    lat_all, key_cot = lax.optimization_barrier((lat_all, key_cot))
    key_seq = lax.all_to_all(key_cot.reshape(count, length, LANES), SP, 0, 0, tiled=True)
    bias_mine = lax.dynamic_index_in_dim(gate_bias.reshape(2, 4, 4, LANES), zh, 1, False)
    *parts, up_send, bias_term = gate_stage(
        zh.astype(jnp.int32).reshape(1), gate_mid, lat_all, up_rows, bias_mine.reshape(8, LANES)
    )
    far, ahead, behind = (turned(parts[k], "zh", k) for k in (2, 1, 3))
    parts = [parts[0], far, ahead, behind]
    bias_row = lax.dynamic_update_slice_in_dim(
        jnp.zeros((2, 4, 4, LANES), F32), bias_term.reshape(2, 1, 4, LANES), zh, 1
    ).reshape(count, 1, LANES)
    slope_grad, conv_term = key_stage(key_seq, projected, before, conv_weight)
    parts, conv_term = lax.optimization_barrier((parts, conv_term))
    send, latent_grad = pack_stage(inputs, parts, conv_term, bias_row, up_send)

    following = lax.ppermute(slope_grad[:8], SP, [(i + 1, i) for i in range(count - 1)])
    plane = jnp.sum(lax.all_to_all(send, PLANE, 0, 0, tiled=True).astype(F32), axis=0)
    rows_share, own_up = rows_down // 4, rows_up // 2
    mixed = rows_share + CONV + 1
    same = (jnp.arange(4) == zh).reshape(4, 1, 1, 1)
    to_heads = jnp.where(same, plane[: 4 * own_up].reshape(1, 4, own_up, LANES), 0.0)
    to_all = jnp.broadcast_to(plane[4 * own_up : 4 * own_up + mixed], (4, 4, mixed, LANES))
    line = jnp.concatenate([to_heads, to_all], axis=2).astype(BF16)
    line = lax.all_to_all(
        line.reshape(16, own_up + mixed, LANES), ("zh", "zl"), 0, 0, tiled=True
    )
    input_grad = input_stage(
        slope_grad, following, conv_weight, key_full, latent_grad, down_full
    )[None]
    line, input_grad = lax.optimization_barrier((line, input_grad))
    done = jnp.sum(line.astype(F32), axis=0) * float(65536) ** (-0.5)
    shares = lax.all_to_all(
        jnp.broadcast_to(done[None], (4,) + done.shape), ("xl", "dp"), 0, 0, tiled=True
    )

    at = lax.axis_index("xl").astype(jnp.int32).reshape(1)
    down_own, up_own, conv_own, bias_own = finish_stage(at, shares, rows_down, rows_up)
    return input_grad, down_own, up_own, conv_own, bias_own.reshape(4 * LANES)


def solution(mesh):
    fine = Mesh(mesh.devices.reshape(2, 4, 4, 8, 2), ("xl", "zh", "zl", "fsdp", "dp"))
    windows = ("fsdp", "dp")
    return jax.shard_map(
        per_device,
        mesh=fine,
        in_specs=(
            P(windows, SP, None),
            P(windows, SP, None),
            P(windows, None, SP),
            P(windows, None, SP),
            P("fsdp", None),
            P("fsdp", None),
            P("fsdp", None),
            P(),
            P(),
        ),
        out_specs=(
            P(windows, SP, None),
            P("fsdp", None),
            P("fsdp", SP),
            P(None, "fsdp"),
            P("fsdp"),
        ),
        check_vma=False,
    )
```
